32 devices in a mesh: probe: 2 (over x), row: 4 (over y, core), col: 4 (over z).
Axes of the slice: x: 2, y: 2, z: 4, core: 2. Of those that a mesh axis runs over, the one named last changes fastest.
Arguments:
- flow_state: bfloat16 [2, 5, 192, 192, 384], P('probe', None, 'row', 'col'), may hold values from -6 to 6
- forcing: bfloat16 [2, 5, 192, 192, 384], P('probe', None, 'row', 'col'), may hold values from -6 to 6
- advect_x: bfloat16 [192, 192, 384], P('row', 'col'), may hold values from 0.19921875 to 1.5
- advect_y: bfloat16 [192, 192, 384], P('row', 'col'), may hold values from 0.19921875 to 1.5
- advect_z: bfloat16 [192, 192, 384], P('row', 'col'), may hold values from 0.19921875 to 1.5
- diffusivity: float32 [5], replicated, may hold values from 0.2 to 1
- deriv_x: bfloat16 [2, 384, 384], replicated, may hold values from -0.3125 to 0.3125
- deriv_y: bfloat16 [2, 192, 192], replicated, may hold values from -0.4375 to 0.4375
- deriv_z: bfloat16 [2, 192, 192], replicated, may hold values from -0.4375 to 0.4375
- test_mix: float32 [2, 2], replicated, may hold values from -4 to 4
Outputs:
- section_out: bfloat16 [2, 5, 192, 192, 384], P('probe', None, 'row', 'col')
- sketch: bfloat16 [2, 5, 192, 192, 384], P(None, None, 'row', 'col', 'probe')
The draws below stay inside these ranges and needn't reach their ends.
All inputs are finite; a program needn't handle non-finite values.
Results may differ from the reference program's by a relative error of at most 0.0095.
Values may be sent and summed in bfloat16 or wider, within the bound.
A program may use at most 256 MiB of HBM per device.

```python
import math
import jax
import jax.numpy as jnp
from jax import lax

NX = 384
NY = 192
NZ = 192
VARS = 5
FRC_DEV = 1
FORCINGS = 2
N_PROBE = 2


def block_levels(rng, dims, cuts, low, largest):
    level, own = 1.0, jax.random.fold_in(rng, 6)
    for position, shards_of in cuts:
        steps = jnp.exp(jax.random.uniform(jax.random.fold_in(own, position), (shards_of,), jnp.float32, low / len(cuts), largest / len(cuts)))
        level = level * jnp.repeat(steps, dims[position] // shards_of).reshape([-1 if axis == position else 1 for axis in range(len(dims))])
    return level


def normal_values(rng, shape, scale, bound, shards=(), held_as=jnp.bfloat16):
    factor_of = block_levels(rng, shape, shards, -0.22, 0.18) if shards else 1.0
    result = jax.random.normal(rng, shape, jnp.float32) * scale * factor_of
    return jnp.minimum(jnp.maximum(result, -bound), bound).astype(held_as)


def setup_inputs(seed: int = 0) -> dict:
    seeds = jax.random.split(jax.random.key(seed), 11)
    return {
        "flow_state": normal_values(seeds[0], (FORCINGS, VARS, NY, NZ, NX), 1.0, 6.0, ((0, 2), (2, 4), (3, 4))),
        "forcing": normal_values(seeds[1], (FORCINGS, VARS, NY, NZ, NX), 1.0, 6.0, ((0, 2), (2, 4), (3, 4))),
        "advect_x": jnp.clip(0.19921875 + 1.3007812 * jax.random.uniform(seeds[2], (NY, NZ, NX), jnp.float32) ** block_levels(seeds[2], (NY, NZ, NX), ((0, 4), (1, 4)), -0.2, 0.2), 0.19921875, 1.5).astype(jnp.bfloat16),
        "advect_y": jnp.clip(0.19921875 + 1.3007812 * jax.random.uniform(seeds[3], (NY, NZ, NX), jnp.float32) ** block_levels(seeds[3], (NY, NZ, NX), ((0, 4), (1, 4)), -0.2, 0.2), 0.19921875, 1.5).astype(jnp.bfloat16),
        "advect_z": jnp.clip(0.19921875 + 1.3007812 * jax.random.uniform(seeds[4], (NY, NZ, NX), jnp.float32) ** block_levels(seeds[4], (NY, NZ, NX), ((0, 4), (1, 4)), -0.2, 0.2), 0.19921875, 1.5).astype(jnp.bfloat16),
        "diffusivity": jnp.clip(jnp.exp(jax.random.uniform(seeds[5], (VARS,), jnp.float32, math.log(0.2), math.log(1.0))), 0.2, 1.0),
        "deriv_x": normal_values(seeds[6], (2, NX, NX), NX ** -0.5, 0.3125),
        "deriv_y": normal_values(seeds[7], (2, NY, NY), NY ** -0.5, 0.4375),
        "deriv_z": normal_values(seeds[8], (2, NZ, NZ), NZ ** -0.5, 0.4375),
        "test_mix": normal_values(seeds[9], (FORCINGS, FORCINGS), FORCINGS ** -0.5, 4.0, (), jnp.float32),
    }


step_size = 0.25


def reference(flow_state, forcing, advect_x, advect_y, advect_z, diffusivity, deriv_x, deriv_y, deriv_z, test_mix):
    mat_x = deriv_x.astype(jnp.float32)
    mat_y = deriv_y.astype(jnp.float32)
    mat_z = deriv_z.astype(jnp.float32)
    vel_x = advect_x.astype(jnp.float32)
    vel_y = advect_y.astype(jnp.float32)
    vel_z = advect_z.astype(jnp.float32)
    sections = []
    for f in range(FORCINGS):
        per_var = []
        for v in range(VARS):
            field_f32 = flow_state[f, v].astype(jnp.float32)
            coeff = diffusivity[v]
            grad_x = jnp.einsum("yzj,kij->kyzi", field_f32, mat_x)
            term_x = -vel_x * grad_x[0] + coeff * grad_x[1]
            grad_y = jnp.einsum("jzx,kij->kizx", field_f32, mat_y)
            term_y = (-vel_y * grad_y[0] + coeff * grad_y[1]).astype(jnp.bfloat16)
            term_y = lax.optimization_barrier(term_y).astype(jnp.float32)
            grad_z = jnp.einsum("yjx,kij->kyix", field_f32, mat_z)
            term_z = (-vel_z * grad_z[0] + coeff * grad_z[1]).astype(jnp.bfloat16)
            term_z = lax.optimization_barrier(term_z).astype(jnp.float32)
            total_rhs = term_x + term_y + term_z + forcing[f, v].astype(jnp.float32)
            per_var.append((field_f32 + step_size * total_rhs).astype(jnp.bfloat16))
        sections.append(jnp.stack(per_var))
    section_out = jnp.stack(sections)
    columns = []
    for g in range(FORCINGS):
        summed = jnp.zeros(section_out.shape[1:], jnp.float32)
        for h in range(N_PROBE):
            group_sum = jnp.zeros(section_out.shape[1:], jnp.float32)
            for f in range(h * FRC_DEV, (h + 1) * FRC_DEV):
                group_sum = group_sum + section_out[f].astype(jnp.float32) * test_mix[f, g]
            rounded = lax.optimization_barrier(group_sum.astype(jnp.bfloat16))
            summed = summed + rounded.astype(jnp.float32)
        columns.append(summed.astype(jnp.bfloat16))
    sketch = jnp.stack(columns)
    return section_out, sketch
```

```python
import jax
import jax.numpy as jnp
from jax import lax
from jax.experimental import pallas as pl
from jax.experimental.pallas import tpu as pltpu
from jax.sharding import PartitionSpec as P

step_size = 0.25
F32, BF16 = jnp.float32, jnp.bfloat16
VMEM_BYTES = 52 * 1024 * 1024
SMEM = pl.BlockSpec(memory_space=pltpu.SMEM)


def params():
    return pltpu.CompilerParams(vmem_limit_bytes=VMEM_BYTES)


def cost(flops, nbytes):
    return pl.CostEstimate(flops=flops, bytes_accessed=nbytes, transcendentals=0)


def xy_kernel(coef, state, forcing, adv_x, adv_y, lines, mat_x, mat_y, out):
    _, ny, zb, nx = state.shape
    rows = ny * zb
    c = coef[pl.program_id(1)]
    own = state[...].reshape(rows, nx)
    gx = jnp.dot(own, mat_x[...], preferred_element_type=F32)
    total = c * gx[:, nx:] - adv_x[...].reshape(rows, nx).astype(F32) * gx[:, :nx]
    gy = jnp.dot(mat_y[...], lines[...].reshape(mat_y.shape[1], nx), preferred_element_type=F32)
    total += c * gy[rows:] - adv_y[...].reshape(rows, nx).astype(F32) * gy[:rows]
    total += forcing[...].reshape(rows, nx).astype(F32)
    out[...] = (own.astype(F32) + step_size * total).reshape(out.shape)


def z_kernel(v, coef, lines, adv, mat_z, out):
    n, yb, nz, nx = lines.shape
    full = n * nz
    c = coef[v]
    for y in range(yb):
        g = jnp.dot(mat_z[...], lines[:, y].reshape(full, nx), preferred_element_type=F32)
        term = c * g[full:] - adv[:, y].reshape(full, nx).astype(F32) * g[:full]
        out[:, y] = term.astype(BF16).reshape(n, nz, nx)


def combine_kernel(me, pre, back, *refs):
    section, own, send = refs[-3:]
    total = (pre[0] + step_size * back[...].astype(F32)).astype(BF16)
    section[0] = total
    part = own.shape[-1]
    n = total.shape[-1] // part
    pieces = [total[..., k * part : (k + 1) * part] for k in range(n)]

    @pl.when(me[0] == 0)
    def _():
        own[...] = pieces[0]
        for s in range(1, n):
            send[s - 1] = pieces[s]

    for p in range(1, n):
        @pl.when(me[0] == p)
        def _(p=p):
            own[...] = pieces[p]
            for s in range(1, n):
                send[s - 1] = pieces[(p + s) % n]


def sketch_kernel(mix, own, got, *refs):
    out = refs[-1]
    for g in range(out.shape[0]):
        total = (own[...].astype(F32) * mix[0, g]).astype(BF16).astype(F32)
        for s in range(got.shape[0]):
            total += (got[s].astype(F32) * mix[s + 1, g]).astype(BF16).astype(F32)
        out[g, 0] = total.astype(BF16)


def on_device(flow_state, forcing, advect_x, advect_y, advect_z, diffusivity, deriv_x, deriv_y, deriv_z, test_mix):
    frc_dev, nvars, ny, nz, nx = flow_state.shape
    assert frc_dev == 1
    n_row, n_col, n_probe = lax.axis_size("row"), lax.axis_size("col"), lax.axis_size("probe")
    columns = test_mix.shape[1]
    part = nx // n_probe
    yb = -(-ny // n_col)
    spare = yb * n_col - ny
    state, force = flow_state[0], forcing[0]
    probe = lax.axis_index("probe")

    def exchange(block):
        return lax.all_to_all(block, "col", split_axis=0, concat_axis=0)

    def divided(block):
        if spare:
            block = jnp.pad(block, ((0, spare), (0, 0), (0, 0)))
        return block.reshape(n_col, yb, nz, nx)

    adv_z = exchange(divided(advect_z))
    lines_z = [exchange(divided(state[v])) for v in range(nvars)]
    lines_y = lax.all_gather(state, "row")

    zb = 16 if nz % 16 == 0 else nz
    own_rows = lax.dynamic_slice_in_dim(deriv_y, lax.axis_index("row") * ny, ny, 1)
    own_rows = own_rows.reshape(2 * ny, n_row * ny)
    tall, wide = 2 * ny * zb, n_row * ny * zb
    spread_rows = (jnp.arange(tall)[:, None] // zb == jnp.arange(2 * ny)[None]).astype(BF16)
    spread_cols = (jnp.arange(n_row * ny)[:, None] == jnp.arange(wide)[None] // zb).astype(BF16)
    mat_y = jnp.dot(spread_rows, own_rows, preferred_element_type=BF16)
    mat_y = jnp.dot(mat_y, spread_cols, preferred_element_type=BF16)
    same_z = jnp.arange(tall)[:, None] % zb == jnp.arange(wide)[None] % zb
    mat_y = jnp.where(same_z, mat_y, jnp.zeros((), BF16))
    mat_x = deriv_x.reshape(2 * nx, nx).T
    mat_z = deriv_z.reshape(2 * n_col * nz, n_col * nz)

    block = ny * nz * nx
    one = pl.BlockSpec((1, ny, zb, nx), lambda z, v: (v, 0, z, 0))
    adv = pl.BlockSpec((ny, zb, nx), lambda z, v: (0, z, 0))
    pre = pl.pallas_call(
        xy_kernel,
        grid=(nz // zb, nvars),
        in_specs=[
            SMEM, one, one, adv, adv,
            pl.BlockSpec((n_row, 1, ny, zb, nx), lambda z, v: (0, v, 0, z, 0)),
            pl.BlockSpec(mat_x.shape, lambda z, v: (0, 0), pipeline_mode=pl.Buffered(1)),
            pl.BlockSpec(mat_y.shape, lambda z, v: (0, 0), pipeline_mode=pl.Buffered(1)),
        ],
        out_specs=one,
        out_shape=jax.ShapeDtypeStruct(state.shape, F32),
        compiler_params=params(),
        cost_estimate=cost(nvars * block * (4 * nx + 4 * n_row * ny * zb), nvars * block * (8 + 2 * n_row)),
        name="xy_terms",
    )(diffusivity, state, force, advect_x, advect_y, lines_y, mat_x, mat_y)

    ys = next(k for k in (4, 3, 2, 1) if yb % k == 0)
    z_spec = pl.BlockSpec((n_col, ys, nz, nx), lambda y: (0, y, 0, 0))
    back = []
    for v in range(nvars):
        term = pl.pallas_call(
            lambda *refs, v=v: z_kernel(v, *refs),
            grid=(yb // ys,),
            in_specs=[SMEM, z_spec, z_spec, pl.BlockSpec(mat_z.shape, lambda y: (0, 0))],
            out_specs=z_spec,
            out_shape=jax.ShapeDtypeStruct((n_col, yb, nz, nx), BF16),
            compiler_params=params(),
            cost_estimate=cost(block * 4 * n_col * nz, block * 6),
            name="z_terms",
        )(diffusivity, lines_z[v], adv_z, mat_z)
        back.append(exchange(term).reshape(n_col * yb, nz, nx)[:ny])

    yc = next(k for k in (12, 8, 6, 4, 3, 2, 1) if ny % k == 0)
    mix = jnp.stack([test_mix[lax.rem(probe - s + n_probe, n_probe)] for s in range(n_probe)])
    me = probe.reshape(1)
    section, owns, gots = None, [], []
    any_spec = pl.BlockSpec(memory_space=pl.ANY)
    for v in range(nvars):
        carried = [] if section is None else [section]
        section, own, send = pl.pallas_call(
            combine_kernel,
            grid=(ny // yc,),
            in_specs=[
                SMEM,
                pl.BlockSpec((1, yc, nz, nx), lambda y, v=v: (v, y, 0, 0)),
                pl.BlockSpec((yc, nz, nx), lambda y: (y, 0, 0)),
            ] + [any_spec] * len(carried),
            out_specs=[
                pl.BlockSpec((1, yc, nz, nx), lambda y, v=v: (v, y, 0, 0)),
                pl.BlockSpec((yc, nz, part), lambda y: (y, 0, 0)),
                pl.BlockSpec((n_probe - 1, yc, nz, part), lambda y: (0, y, 0, 0)),
            ],
            out_shape=[
                jax.ShapeDtypeStruct(state.shape, BF16),
                jax.ShapeDtypeStruct((ny, nz, part), BF16),
                jax.ShapeDtypeStruct((n_probe - 1, ny, nz, part), BF16),
            ],
            input_output_aliases={3: 0} if carried else {},
            compiler_params=params(),
            cost_estimate=cost(block * 2, block * 10),
            name="combine",
        )(me, pre, back[v], *carried)
        got = [
            lax.ppermute(send[s - 1], "probe", [(p, (p + s) % n_probe) for p in range(n_probe)])
            for s in range(1, n_probe)
        ]
        owns.append(own)
        gots.append(got[0][None] if n_probe == 2 else jnp.stack(got))

    sketch = None
    for v in range(nvars):
        carried = [] if sketch is None else [sketch]
        sketch = pl.pallas_call(
            sketch_kernel,
            grid=(ny // yc,),
            in_specs=[
                SMEM,
                pl.BlockSpec((yc, nz, part), lambda y: (y, 0, 0)),
                pl.BlockSpec((n_probe - 1, yc, nz, part), lambda y: (0, y, 0, 0)),
            ] + [any_spec] * len(carried),
            out_specs=pl.BlockSpec((columns, 1, yc, nz, part), lambda y, v=v: (0, v, y, 0, 0)),
            out_shape=jax.ShapeDtypeStruct((columns, nvars, ny, nz, part), BF16),
            input_output_aliases={3: 0} if carried else {},
            compiler_params=params(),
            cost_estimate=cost(block * 4, block * 4),
            name="sketch_columns",
        )(mix, owns[v], gots[v], *carried)
    return (section[None], sketch)


def solution(mesh):
    placed = (
        P("probe", None, "row", "col", None),
        P("probe", None, "row", "col", None),
        P("row", "col", None),
        P("row", "col", None),
        P("row", "col", None),
        P(),
        P(),
        P(),
        P(),
        P(),
    )
    return jax.shard_map(
        on_device,
        mesh=mesh,
        in_specs=placed,
        out_specs=(P("probe", None, "row", "col", None), P(None, None, "row", "col", "probe")),
        check_vma=False,
    )
```

```python
import jax
import jax.numpy as jnp
from jax import lax
from jax.experimental import pallas as pl
from jax.experimental.pallas import tpu as pltpu
from jax.sharding import PartitionSpec as P

step_size = 0.25
F32, BF16 = jnp.float32, jnp.bfloat16
VMEM_BYTES = 52 * 1024 * 1024
SMEM = pl.BlockSpec(memory_space=pltpu.SMEM)


def params():
    return pltpu.CompilerParams(vmem_limit_bytes=VMEM_BYTES)


def cost(flops, nbytes):
    return pl.CostEstimate(flops=flops, bytes_accessed=nbytes, transcendentals=0)


def xy_kernel(coef, state, forcing, adv_x, adv_y, lines, mat_x, mat_y, *refs):
    out = refs[-1]
    _, ny, zb, nx = state.shape
    rows = ny * zb
    c = coef[0]
    own = state[...].reshape(rows, nx)
    gx = jnp.dot(own, mat_x[...], preferred_element_type=F32)
    total = c * gx[:, nx:] - adv_x[...].reshape(rows, nx).astype(F32) * gx[:, :nx]
    gy = jnp.dot(mat_y[...], lines[...].reshape(mat_y.shape[1], nx), preferred_element_type=F32)
    total += c * gy[rows:] - adv_y[...].reshape(rows, nx).astype(F32) * gy[:rows]
    total += forcing[...].reshape(rows, nx).astype(F32)
    out[...] = (own.astype(F32) + step_size * total).reshape(out.shape)


def z_kernel(coef, lines, adv, mat_z, *refs):
    out = refs[-1]
    n, yb, nz, nx = lines.shape
    full = n * nz
    c = coef[0]
    for y in range(yb):
        g = jnp.dot(mat_z[...], lines[:, y].reshape(full, nx), preferred_element_type=F32)
        term = c * g[full:] - adv[:, y].reshape(full, nx).astype(F32) * g[:full]
        out[:, y] = term.astype(BF16).reshape(n, nz, nx)


def combine_kernel(me, pre, back, *refs):
    section, own, send = refs[-3:]
    total = (pre[...] + step_size * back[...].astype(F32)).astype(BF16)
    section[0] = total
    part = own.shape[-1]
    n = total.shape[-1] // part
    pieces = [total[..., k * part : (k + 1) * part] for k in range(n)]

    @pl.when(me[0] == 0)
    def _():
        own[...] = pieces[0]
        for s in range(1, n):
            send[s - 1] = pieces[s]

    for p in range(1, n):
        @pl.when(me[0] == p)
        def _(p=p):
            own[...] = pieces[p]
            for s in range(1, n):
                send[s - 1] = pieces[(p + s) % n]


def sketch_kernel(mix, own, got, *refs):
    out = refs[-1]
    for g in range(out.shape[0]):
        total = (own[...].astype(F32) * mix[0, g]).astype(BF16).astype(F32)
        for s in range(got.shape[0]):
            total += (got[s].astype(F32) * mix[s + 1, g]).astype(BF16).astype(F32)
        out[g, 0] = total.astype(BF16)


def on_device(flow_state, forcing, advect_x, advect_y, advect_z, diffusivity, deriv_x, deriv_y, deriv_z, test_mix):
    frc_dev, nvars, ny, nz, nx = flow_state.shape
    assert frc_dev == 1
    n_row, n_col, n_probe = lax.axis_size("row"), lax.axis_size("col"), lax.axis_size("probe")
    columns = test_mix.shape[1]
    part = nx // n_probe
    yb = -(-ny // (n_col * n_probe)) * n_probe
    half = yb // n_probe
    spare = yb * n_col - ny
    state, force = flow_state[0], forcing[0]
    probe = lax.axis_index("probe")

    def exchange(block):
        return lax.all_to_all(block, "col", split_axis=0, concat_axis=0)

    def divided(block):
        if spare:
            block = jnp.pad(block, ((0, spare), (0, 0), (0, 0)))
        return block.reshape(n_col, yb, nz, nx)

    def passed(block, shift):
        return lax.ppermute(block, "probe", [(p, (p + shift) % n_probe) for p in range(n_probe)])

    mine = exchange(lax.dynamic_slice_in_dim(divided(advect_z), probe * half, half, 1))
    adv_z = jnp.zeros((n_col, yb, nz, nx), BF16)
    for s in range(n_probe):
        share = passed(mine, s) if s else mine
        source = lax.rem(probe - s + n_probe, n_probe)
        adv_z = lax.dynamic_update_slice_in_dim(adv_z, share, source * half, 1)
    lines_z = [exchange(divided(state[v])) for v in range(nvars)]
    lines_y = lax.all_gather(state, "row")

    zb = 16 if nz % 16 == 0 else nz
    own_rows = lax.dynamic_slice_in_dim(deriv_y, lax.axis_index("row") * ny, ny, 1)
    own_rows = own_rows.reshape(2 * ny, n_row * ny)
    tall, wide = 2 * ny * zb, n_row * ny * zb
    spread_rows = (jnp.arange(tall)[:, None] // zb == jnp.arange(2 * ny)[None]).astype(BF16)
    spread_cols = (jnp.arange(n_row * ny)[:, None] == jnp.arange(wide)[None] // zb).astype(BF16)
    mat_y = jnp.dot(spread_rows, own_rows, preferred_element_type=BF16)
    mat_y = jnp.dot(mat_y, spread_cols, preferred_element_type=BF16)
    same_z = jnp.arange(tall)[:, None] % zb == jnp.arange(wide)[None] % zb
    mat_y = jnp.where(same_z, mat_y, jnp.zeros((), BF16))
    mat_x = deriv_x.reshape(2 * nx, nx).T
    mat_z = deriv_z.reshape(2 * n_col * nz, n_col * nz)

    block = ny * nz * nx
    any_spec = pl.BlockSpec(memory_space=pl.ANY)
    ys = next(k for k in (4, 3, 2, 1) if yb % k == 0)
    yc = next(k for k in (12, 8, 6, 4, 3, 2, 1) if ny % k == 0)
    z_spec = pl.BlockSpec((n_col, ys, nz, nx), lambda y: (0, y, 0, 0))
    adv = pl.BlockSpec((ny, zb, nx), lambda z: (0, z, 0))
    mix = jnp.stack([test_mix[lax.rem(probe - s + n_probe, n_probe)] for s in range(n_probe)])
    me = probe.reshape(1)

    def z_terms(v, after):
        return pl.pallas_call(
            z_kernel,
            grid=(yb // ys,),
            in_specs=[SMEM, z_spec, z_spec, pl.BlockSpec(mat_z.shape, lambda y: (0, 0))] + [any_spec] * len(after),
            out_specs=z_spec,
            out_shape=jax.ShapeDtypeStruct((n_col, yb, nz, nx), BF16),
            compiler_params=params(),
            cost_estimate=cost(block * 4 * n_col * nz, block * 6),
            name="z_terms",
        )(diffusivity[v : v + 1], lines_z[v], adv_z, mat_z, *after)

    def xy_terms(v, after):
        one = pl.BlockSpec((1, ny, zb, nx), lambda z: (v, 0, z, 0))
        return pl.pallas_call(
            xy_kernel,
            grid=(nz // zb,),
            in_specs=[
                SMEM, one, one, adv, adv,
                pl.BlockSpec((n_row, 1, ny, zb, nx), lambda z: (0, v, 0, z, 0)),
                pl.BlockSpec(mat_x.shape, lambda z: (0, 0), pipeline_mode=pl.Buffered(1)),
                pl.BlockSpec(mat_y.shape, lambda z: (0, 0), pipeline_mode=pl.Buffered(1)),
            ] + [any_spec] * len(after),
            out_specs=adv,
            out_shape=jax.ShapeDtypeStruct((ny, nz, nx), F32),
            compiler_params=params(),
            cost_estimate=cost(block * (4 * nx + 4 * n_row * ny * zb), block * (8 + 2 * n_row)),
            name="xy_terms",
        )(diffusivity[v : v + 1], state, force, advect_x, advect_y, lines_y, mat_x, mat_y, *after)

    def combine(v, pre, back, section):
        carried = [] if section is None else [section]
        whole = pl.BlockSpec((yc, nz, nx), lambda y: (y, 0, 0))
        return pl.pallas_call(
            combine_kernel,
            grid=(ny // yc,),
            in_specs=[SMEM, whole, whole] + [any_spec] * len(carried),
            out_specs=[
                pl.BlockSpec((1, yc, nz, nx), lambda y: (v, y, 0, 0)),
                pl.BlockSpec((yc, nz, part), lambda y: (y, 0, 0)),
                pl.BlockSpec((n_probe - 1, yc, nz, part), lambda y: (0, y, 0, 0)),
            ],
            out_shape=[
                jax.ShapeDtypeStruct(state.shape, BF16),
                jax.ShapeDtypeStruct((ny, nz, part), BF16),
                jax.ShapeDtypeStruct((n_probe - 1, ny, nz, part), BF16),
            ],
            input_output_aliases={3: 0} if carried else {},
            compiler_params=params(),
            cost_estimate=cost(block * 2, block * 10),
            name="combine",
        )(me, pre, back, *carried)

    def sketch_columns(v, own, got, sketch):
        carried = [] if sketch is None else [sketch]
        return pl.pallas_call(
            sketch_kernel,
            grid=(ny // yc,),
            in_specs=[
                SMEM,
                pl.BlockSpec((yc, nz, part), lambda y: (y, 0, 0)),
                pl.BlockSpec((n_probe - 1, yc, nz, part), lambda y: (0, y, 0, 0)),
            ] + [any_spec] * len(carried),
            out_specs=pl.BlockSpec((columns, 1, yc, nz, part), lambda y: (0, v, y, 0, 0)),
            out_shape=jax.ShapeDtypeStruct((columns, nvars, ny, nz, part), BF16),
            input_output_aliases={3: 0} if carried else {},
            compiler_params=params(),
            cost_estimate=cost(block * 4, block * 4),
            name="sketch_columns",
        )(mix, own, got, *carried)

    pres, sends, section, sketch = [], [], None, None
    for v in range(nvars):
        after = lines_z[1 : nvars - 1] if v == 0 else [pres[v - 1]]
        if v == 1:
            after.append(lines_z[-1])
        if v >= 2:
            after.append(sends[v - 2])
        term = z_terms(v, after)
        back = exchange(term).reshape(n_col * yb, nz, nx)[:ny]
        pres.append(xy_terms(v, [term]))
        section, own, send = combine(v, pres[v], back, section)
        sends.append(send)
        got = [passed(send[s - 1], s) for s in range(1, n_probe)]
        got = got[0][None] if n_probe == 2 else jnp.stack(got)
        sketch = sketch_columns(v, own, got, sketch)
    return (section[None], sketch)


def solution(mesh):
    placed = (
        P("probe", None, "row", "col", None),
        P("probe", None, "row", "col", None),
        P("row", "col", None),
        P("row", "col", None),
        P("row", "col", None),
        P(),
        P(),
        P(),
        P(),
        P(),
    )
    return jax.shard_map(
        on_device,
        mesh=mesh,
        in_specs=placed,
        out_specs=(P("probe", None, "row", "col", None), P(None, None, "row", "col", "probe")),
        check_vma=False,
    )
```
